32 devices in a mesh: blocks: 2 (over x), strip: 16 (over z, y, core).
Axes of the slice: x: 2, y: 2, z: 4, core: 2. Of those that a mesh axis runs over, the one named last changes fastest.
Arguments:
- estimate: float32 [128, 256, 256], P(('blocks', 'strip')), parts along dimension 0, may hold values from 0.5 to 2
- views_data: bfloat16 [8, 128, 256, 256], P(None, ('blocks', 'strip')), parts along dimension 1, may hold values from 0.02 to 30, as said below
- kernel_x: float32 [8, 9], replicated, may hold values from 0.1 to 1
- kernel_y: float32 [8, 5], replicated, may hold values from 0.1 to 1
- kernel_z: float32 [8, 9], replicated, may hold values from 0.1 to 1
Outputs:
- deconvolved: float32 [128, 256, 256], P(('blocks', 'strip')), parts along dimension 0
The draws below stay inside these ranges and needn't reach their ends.
There are 2 independent parts, one for each index of `blocks`. The reference program is written for one: setup_inputs(seed, part) draws one part's arguments, and reference() takes and returns one part's arrays. A program takes and returns all parts, laid end to end along the dimension named above; an argument that names none is the same for every part. Nothing has to cross between parts.
Inputs may be any that keep to these rules, and one draw needn't show every extreme that they name: `views_data`: positive recorded intensities of each view.
All inputs are finite; a program needn't handle non-finite values.
Results may differ from the reference program's by a relative error of at most 0.00067.
Values may be sent and summed in bfloat16 or wider, within the bound.
A program may use at most 128 MiB of HBM per device.

```python
import math
import jax
import jax.numpy as jnp
from jax import lax

VIEWS = 8
X = 256
Z = 256
ITERS = 2
RX = 4
RY = 2
RZ = 4
NY = 64


def draw_views_data(key, part):
    keys = jax.random.split(jax.random.fold_in(key, 11), 3)
    shape = (VIEWS, NY, X, Z)
    base = jnp.exp(jax.random.uniform(keys[0], shape, jnp.float32, math.log(0.3), math.log(3.0)))
    gains = jnp.exp(jax.random.uniform(keys[1], (VIEWS,), jnp.float32, -0.7, 0.7))
    slopes = jax.random.uniform(keys[2], (VIEWS,), jnp.float32, -0.4, 1.5)
    ypos = jnp.arange(NY, dtype=jnp.float32) / NY
    trend = (1.0 + 4.0 * ypos)[None, :] * (1.0 + slopes[:, None] * ypos[None, :]) / 4.0
    values = base * gains[:, None, None, None] * trend[:, :, None, None]
    return values.astype(jnp.bfloat16)


def levels(own_key, shape, pieces, low, top_value):
    factor_of, own = 1.0, jax.random.fold_in(own_key, 6)
    for position, shards_of in pieces:
        steps = jnp.exp(jax.random.uniform(jax.random.fold_in(own, position), (shards_of,), jnp.float32, low / len(pieces), top_value / len(pieces)))
        factor_of = factor_of * jnp.repeat(steps, shape[position] // shards_of).reshape([-1 if axis == position else 1 for axis in range(len(shape))])
    return factor_of


def setup_inputs(seed: int = 0, part: int = 0) -> dict:
    key_list = jax.random.split(jax.random.key(seed), 6)
    own_keys = jax.random.split(jax.random.fold_in(key_list[5], part), 6)
    estimate = jnp.clip(jnp.exp(math.log(2.0) - 1.3862944 * jax.random.uniform(own_keys[0], (NY, X, Z), jnp.float32) ** levels(own_keys[0], (NY, X, Z), ((0, 16),), -0.2, 0.2)), 0.5, 2.0)
    views_data = draw_views_data(jax.random.fold_in(jax.random.fold_in(key_list[5], part), 71), part)
    kernel_x = jnp.clip(jnp.exp(jax.random.uniform(key_list[2], (VIEWS, 2 * RX + 1), jnp.float32, math.log(0.1), math.log(1.0))), 0.1, 1.0)
    kernel_y = jnp.clip(jnp.exp(jax.random.uniform(key_list[3], (VIEWS, 2 * RY + 1), jnp.float32, math.log(0.1), math.log(1.0))), 0.1, 1.0)
    kernel_z = jnp.clip(jnp.exp(jax.random.uniform(key_list[4], (VIEWS, 2 * RZ + 1), jnp.float32, math.log(0.1), math.log(1.0))), 0.1, 1.0)
    return {"estimate": estimate, "views_data": views_data, "kernel_x": kernel_x, "kernel_y": kernel_y, "kernel_z": kernel_z}


def rounded(value):
    return lax.optimization_barrier(value.astype(jnp.bfloat16)).astype(jnp.float32)


def shifted(field, kernel, along, radius, mirror):
    length = field.shape[along]
    widths = [(0, 0)] * field.ndim
    widths[along] = (radius, radius)
    padded = jnp.pad(field, widths)
    total = jnp.zeros(field.shape, jnp.float32)
    for offset in range(2 * radius + 1):
        start = 2 * radius - offset if mirror else offset
        piece = lax.slice_in_dim(padded, start, start + length, axis=along)
        total = total + kernel[offset] * piece
    return total


def blurring(field, prof_y, prof_x, prof_z, mirror):
    first = rounded(shifted(field, prof_y, 0, RY, mirror))
    second = rounded(shifted(first, prof_x, 1, RX, mirror))
    return shifted(second, prof_z, 2, RZ, mirror)


def reference(estimate, views_data, kernel_x, kernel_y, kernel_z):
    norm_y = kernel_y / jnp.sum(kernel_y, axis=1, keepdims=True)
    norm_x = rounded(kernel_x / jnp.sum(kernel_x, axis=1, keepdims=True))
    norm_z = rounded(kernel_z / jnp.sum(kernel_z, axis=1, keepdims=True))
    totals = jnp.stack([jnp.sum(views_data[view].astype(jnp.float32)) for view in range(VIEWS)])
    weights = jnp.sum(totals) / (VIEWS * totals)
    for step in range(ITERS):
        image = rounded(estimate)
        logsum = jnp.zeros(estimate.shape, jnp.float32)
        for view in range(VIEWS):
            blurred = blurring(image, norm_y[view], norm_x[view], norm_z[view], False)
            ratio = rounded(weights[view] * views_data[view].astype(jnp.float32) / blurred)
            correction = blurring(ratio, norm_y[view], norm_x[view], norm_z[view], True)
            logsum = logsum + jnp.log(correction)
        estimate = estimate * jnp.exp(logsum / VIEWS)
    return estimate
```

```python
import functools

import jax
import jax.numpy as jnp
from jax import lax
from jax.experimental import pallas as pl
from jax.experimental.pallas import tpu as pltpu
from jax.sharding import PartitionSpec as P

ITERS = 2
CHUNK = 16
MESH = pl.DeviceIdType.MESH
BF = jnp.bfloat16
F32 = jnp.float32


def band(taps_ref, view, length, radius, start, size, flip):
    rows = lax.broadcasted_iota(jnp.int32, (size, length), 0) + start
    columns = lax.broadcasted_iota(jnp.int32, (size, length), 1)
    place = (rows - columns if flip else columns - rows) + radius
    total = jnp.zeros((size, length), F32)
    for t in range(2 * radius + 1):
        total = jnp.where(place == t, taps_ref[view, t], total)
    return total.astype(BF)


def along_y(rows, taps, mirror):
    width = len(taps)
    outs = []
    for o in range(len(rows) - width + 1):
        terms = [
            taps[width - 1 - t if mirror else t] * rows[o + t] for t in range(width)
        ]
        while len(terms) > 1:
            terms = [a + b for a, b in zip(terms[::2], terms[1::2])] + (
                terms[-1:] if len(terms) % 2 else []
            )
        outs.append(terms[0])
    return outs


def dot(a, b):
    return jnp.dot(a, b, preferred_element_type=F32)


def kernel(
    strips, nx, ny, nz, est, data, out,
    img, wide, ax, axt, bz, bzt, fy, ratio, acc,
    local_sem, img_send, img_recv, data_send, data_recv,
):
    views, own, length_x, length_z = data.shape
    ry = (ny.shape[1] - 1) // 2
    rx = (nx.shape[1] - 1) // 2
    rz = (nz.shape[1] - 1) // 2
    halo = 2 * ry
    inner = own + 2 * ry
    me = lax.axis_index("strip")
    has = (me > 0, me < strips - 1)
    peer = (me - 1, me + 1)

    barrier = pltpu.get_barrier_semaphore()
    for side in range(2):
        @pl.when(has[side])
        def _():
            pl.semaphore_signal(
                barrier, inc=1, device_id={"strip": peer[side]}, device_id_type=MESH
            )

    fetch = pltpu.make_async_copy(data, wide.at[:, ry : ry + own], local_sem)
    fetch.start()
    img[0, halo : halo + own] = est[...].astype(BF)
    for side in range(2):
        at_image = slice(0, halo) if side == 0 else slice(halo + own, 2 * halo + own)
        at_data = slice(0, ry) if side == 0 else slice(ry + own, 2 * ry + own)

        @pl.when(jnp.logical_not(has[side]))
        def _():
            for step in range(ITERS):
                img[step, at_image] = jnp.zeros((halo, length_x, length_z), BF)
            wide[:, at_data] = jnp.zeros((views, ry, length_x, length_z), BF)

    def image_copy(step, side):
        if side == 0:
            source, target = pl.ds(halo, halo), pl.ds(halo + own, halo)
        else:
            source, target = pl.ds(own, halo), pl.ds(0, halo)
        return pltpu.make_async_remote_copy(
            src_ref=img.at[step, source],
            dst_ref=img.at[step, target],
            send_sem=img_send.at[step, side],
            recv_sem=img_recv.at[step, 1 - side],
            device_id={"strip": peer[side]},
            device_id_type=MESH,
        )

    def data_copy(view, side):
        if side == 0:
            source, target = pl.ds(0, ry), pl.ds(ry + own, ry)
        else:
            source, target = pl.ds(own - ry, ry), pl.ds(0, ry)
        return pltpu.make_async_remote_copy(
            src_ref=data.at[view, source],
            dst_ref=wide.at[view, target],
            send_sem=data_send.at[side, view],
            recv_sem=data_recv.at[1 - side, view],
            device_id={"strip": peer[side]},
            device_id_type=MESH,
        )

    pl.semaphore_wait(
        barrier, jnp.where(has[0], 1, 0) + jnp.where(has[1], 1, 0)
    )
    for side in range(2):
        @pl.when(has[side])
        def _():
            image_copy(0, side).start()

    @pl.loop(0, views)
    def _(view):
        for side in range(2):
            @pl.when(has[side])
            def _():
                data_copy(view, side).start()

    @pl.loop(0, views)
    def _(view):
        for chunk in range(0, length_x, 64):
            at = pl.ds(chunk, 64)
            ax[view, at] = band(nx, view, length_x, rx, chunk, 64, False)
            axt[view, at] = band(nx, view, length_x, rx, chunk, 64, True)
        for chunk in range(0, length_z, 64):
            at = pl.ds(chunk, 64)
            bz[view, at] = band(nz, view, length_z, rz, chunk, 64, True)
            bzt[view, at] = band(nz, view, length_z, rz, chunk, 64, False)

    fetch.wait()

    for step in range(ITERS):
        for side in range(2):
            @pl.when(has[side])
            def _():
                image_copy(step, 1 - side).wait_recv()

        acc[...] = jnp.zeros_like(acc)

        @pl.loop(0, views)
        def _(view):
            taps = [
                jnp.full((CHUNK, length_z), ny[view, t], F32).astype(BF)
                for t in range(2 * ry + 1)
            ]

            @pl.loop(0, length_x // CHUNK, unroll=2)
            def _(chunk):
                at = pl.ds(pl.multiple_of(chunk * CHUNK, CHUNK), CHUNK)
                rows = [img[step, j, at, :] for j in range(own + 2 * halo)]
                for o, value in enumerate(along_y(rows, taps, False)):
                    fy[o, at, :] = value

            if step == 0:
                for side in range(2):
                    @pl.when(has[side])
                    def _():
                        data_copy(view, 1 - side).wait_recv()

            for o in range(inner):
                second = dot(ax[view], fy[o]).astype(BF)
                blurred = dot(second, bz[view])
                ratio[o] = wide[view, o] * pl.reciprocal(blurred, approx=True).astype(BF)

            @pl.loop(0, length_x // CHUNK, unroll=2)
            def _(chunk):
                at = pl.ds(pl.multiple_of(chunk * CHUNK, CHUNK), CHUNK)
                rows = [ratio[j, at, :] for j in range(inner)]
                for o, value in enumerate(along_y(rows, taps, True)):
                    fy[o, at, :] = value

            for o in range(own):
                second = dot(axt[view], fy[o]).astype(BF)
                acc[o] += jnp.log(dot(second, bzt[view]))

        before = est if step == 0 else out
        out[...] = before[...] * jnp.exp(acc[...] * (1.0 / views))
        if step < ITERS - 1:
            img[step + 1, halo : halo + own] = out[...].astype(BF)
            for side in range(2):
                @pl.when(has[side])
                def _():
                    image_copy(step + 1, side).start()

    for side in range(2):
        @pl.when(has[side])
        def _():
            for step in range(ITERS):
                image_copy(step, side).wait_send()

            @pl.loop(0, views)
            def _(view):
                data_copy(view, side).wait_send()


def local(strips, estimate, views_data, kernel_x, kernel_y, kernel_z):
    views, own, length_x, length_z = views_data.shape
    norm_x, norm_y, norm_z = (
        k / jnp.sum(k, axis=1, keepdims=True) for k in (kernel_x, kernel_y, kernel_z)
    )
    ry = (kernel_y.shape[1] - 1) // 2
    inner = own + 2 * ry
    smem = pl.BlockSpec(memory_space=pltpu.SMEM)
    vmem = pl.BlockSpec(memory_space=pltpu.VMEM)
    plane = (length_x, length_z)
    flops = ITERS * views * (inner + own) * 2 * length_x * length_z * (length_x + length_z)
    unweighted = pl.pallas_call(
        functools.partial(kernel, strips),
        out_shape=jax.ShapeDtypeStruct(estimate.shape, F32),
        in_specs=[smem, smem, smem, vmem, pl.BlockSpec(memory_space=pl.ANY)],
        out_specs=vmem,
        scratch_shapes=[
            pltpu.VMEM((ITERS, own + 4 * ry) + plane, BF),
            pltpu.VMEM((views, inner) + plane, BF),
            pltpu.VMEM((views, length_x, length_x), BF),
            pltpu.VMEM((views, length_x, length_x), BF),
            pltpu.VMEM((views, length_z, length_z), BF),
            pltpu.VMEM((views, length_z, length_z), BF),
            pltpu.VMEM((inner,) + plane, BF),
            pltpu.VMEM((inner,) + plane, BF),
            pltpu.VMEM((own,) + plane, F32),
            pltpu.SemaphoreType.DMA,
            pltpu.SemaphoreType.DMA((ITERS, 2)),
            pltpu.SemaphoreType.DMA((ITERS, 2)),
            pltpu.SemaphoreType.DMA((2, views)),
            pltpu.SemaphoreType.DMA((2, views)),
        ],
        compiler_params=pltpu.CompilerParams(
            collective_id=0, has_side_effects=True, vmem_limit_bytes=44 * 1024 * 1024
        ),
        cost_estimate=pl.CostEstimate(
            flops=flops, bytes_accessed=8 * 1024 * 1024, transcendentals=0
        ),
    )(norm_x, norm_y, norm_z, estimate, views_data)
    totals = lax.psum(jnp.sum(views_data, axis=(1, 2, 3), dtype=F32), "strip")
    log_weights = jnp.log(jnp.sum(totals) / (views * totals))
    return unweighted * jnp.exp(jnp.sum(log_weights) / views)


def solution(mesh):
    placed = (
        P(("blocks", "strip"), None, None),
        P(None, ("blocks", "strip"), None, None),
        P(),
        P(),
        P(),
    )
    return jax.shard_map(
        functools.partial(local, mesh.shape["strip"]),
        mesh=mesh,
        in_specs=placed,
        out_specs=P(("blocks", "strip"), None, None),
        check_vma=False,
    )
```

```python
import functools

import jax
import jax.numpy as jnp
from jax import lax
from jax.experimental import pallas as pl
from jax.experimental.pallas import tpu as pltpu
from jax.sharding import PartitionSpec as P

ITERS = 2
CHUNK = 16
BLOCK = 64
AHEAD = 2
MESH = pl.DeviceIdType.MESH
BF = jnp.bfloat16
F32 = jnp.float32
KINDS = (F32, BF)


def normalised(taps_ref, view):
    taps = [taps_ref[view, t] for t in range(taps_ref.shape[1])]
    total = taps[0]
    for tap in taps[1:]:
        total = total + tap
    return [tap / total for tap in taps]


def band(taps, length, radius, start, size, flip):
    rows = lax.broadcasted_iota(jnp.int32, (size, length), 0) + start
    columns = lax.broadcasted_iota(jnp.int32, (size, length), 1)
    place = (rows - columns if flip else columns - rows) + radius
    total = jnp.zeros((size, length), F32)
    for t in range(2 * radius + 1):
        total = jnp.where(place == t, taps[t], total)
    return total.astype(BF)


def along_y(rows, taps, mirror):
    width = len(taps)
    outs = []
    for o in range(len(rows) - width + 1):
        terms = [
            taps[width - 1 - t if mirror else t] * rows[o + t] for t in range(width)
        ]
        while len(terms) > 1:
            terms = [a + b for a, b in zip(terms[::2], terms[1::2])] + (
                terms[-1:] if len(terms) % 2 else []
            )
        outs.append(terms[0])
    return outs


def dot(a, b):
    return jnp.dot(a, b, preferred_element_type=F32)


def kernel(
    strips, nx, ny, nz, est, data, out,
    img, wide, ax, axt, bz, bzt, half, ratio, acc, first, mine, parts,
    local_sem, est_sem, img_send, img_recv, data_send, data_recv, sum_send, sum_recv,
):
    views, own, length_x, length_z = data.shape
    ry = (ny.shape[1] - 1) // 2
    rx = (nx.shape[1] - 1) // 2
    rz = (nz.shape[1] - 1) // 2
    halo = 2 * ry
    inner = own + 2 * ry
    me = lax.axis_index("strip")
    has = (me > 0, me < strips - 1)
    peer = (me - 1, me + 1)

    fetch_first = pltpu.make_async_copy(est, first, est_sem)
    fetch_first.start()
    barrier = pltpu.get_barrier_semaphore()

    @pl.loop(1, strips)
    def _(distance):
        pl.semaphore_signal(
            barrier,
            inc=1,
            device_id={"strip": lax.rem(me + distance, strips)},
            device_id_type=MESH,
        )

    fetch = pltpu.make_async_copy(data, wide.at[:, ry : ry + own], local_sem)
    fetch.start()
    fetch_first.wait()
    img[0, halo : halo + own] = first[...].astype(BF)
    for side in range(2):
        at_image = slice(0, halo) if side == 0 else slice(halo + own, 2 * halo + own)
        at_data = slice(0, ry) if side == 0 else slice(ry + own, 2 * ry + own)

        @pl.when(jnp.logical_not(has[side]))
        def _():
            for step in range(ITERS):
                img[step, at_image] = jnp.zeros((halo, length_x, length_z), BF)
            wide[:, at_data] = jnp.zeros((views, ry, length_x, length_z), BF)

    def image_copy(step, side):
        if side == 0:
            source, target = pl.ds(halo, halo), pl.ds(halo + own, halo)
        else:
            source, target = pl.ds(own, halo), pl.ds(0, halo)
        return pltpu.make_async_remote_copy(
            src_ref=img.at[step, source],
            dst_ref=img.at[step, target],
            send_sem=img_send.at[step, side],
            recv_sem=img_recv.at[step, 1 - side],
            device_id={"strip": peer[side]},
            device_id_type=MESH,
        )

    def data_copy(view, side):
        if side == 0:
            source, target = pl.ds(0, ry), pl.ds(ry + own, ry)
        else:
            source, target = pl.ds(own - ry, ry), pl.ds(0, ry)
        return pltpu.make_async_remote_copy(
            src_ref=data.at[view, source],
            dst_ref=wide.at[view, target],
            send_sem=data_send.at[side, view],
            recv_sem=data_recv.at[1 - side, view],
            device_id={"strip": peer[side]},
            device_id_type=MESH,
        )

    def sum_copy(distance):
        return pltpu.make_async_remote_copy(
            src_ref=mine,
            dst_ref=parts.at[me],
            send_sem=sum_send.at[distance],
            recv_sem=sum_recv.at[distance],
            device_id={"strip": lax.rem(me + distance, strips)},
            device_id_type=MESH,
        )

    pl.semaphore_wait(barrier, strips - 1)
    for side in range(2):
        @pl.when(has[side])
        def _():
            image_copy(0, side).start()

    for view in range(min(AHEAD, views)):
        for side in range(2):
            @pl.when(has[side])
            def _():
                data_copy(view, side).start()

    fetch.wait()

    @pl.loop(0, views)
    def _(view):
        def add(chunk, total):
            at = pl.ds(pl.multiple_of(chunk * 32, 32), 32)
            for o in range(own):
                total = total + wide[view, ry + o, at, :].astype(F32)
            return total

        total = lax.fori_loop(
            0, length_x // 32, add, jnp.zeros((32, length_z), F32), unroll=2
        )
        mine[pl.ds(view, 1), :] = jnp.sum(total, axis=0, keepdims=True)

    @pl.loop(1, strips)
    def _(distance):
        sum_copy(distance).start()

    parts[me] = mine[...]

    @pl.loop(0, views)
    def _(view):
        taps_x, taps_z = normalised(nx, view), normalised(nz, view)
        for chunk in range(0, length_x, 64):
            at = pl.ds(chunk, 64)
            ax[view, at] = band(taps_x, length_x, rx, chunk, 64, False)
            axt[view, at] = band(taps_x, length_x, rx, chunk, 64, True)
        for chunk in range(0, length_z, 64):
            at = pl.ds(chunk, 64)
            bz[view, at] = band(taps_z, length_z, rz, chunk, 64, True)
            bzt[view, at] = band(taps_z, length_z, rz, chunk, 64, False)

    @pl.loop(1, strips)
    def _(distance):
        sum_copy(distance).wait()

    totals = jnp.sum(jnp.sum(parts[...], axis=0), axis=1, keepdims=True)
    weights = jnp.sum(totals, axis=0, keepdims=True) / (views * totals)
    mine[...] = jnp.broadcast_to(weights, mine.shape)

    def y_then_z(source, count, taps, mirror, matrix):
        @pl.loop(0, length_x // BLOCK, unroll=2)
        def _(block):
            starts = [
                pl.multiple_of(block * BLOCK + c, CHUNK) for c in range(0, BLOCK, CHUNK)
            ]
            pieces = []
            for start in starts:
                rows = [source(j, pl.ds(start, CHUNK)) for j in range(count)]
                pieces += [p.astype(BF) for p in along_y(rows, taps, mirror)]
            outs = len(pieces) // len(starts)
            result = dot(jnp.concatenate(pieces, axis=0), matrix).astype(BF)
            for index in range(len(pieces)):
                at = pl.ds(starts[index // outs], CHUNK)
                half[index % outs, at, :] = result[index * CHUNK : (index + 1) * CHUNK]

    for step in range(ITERS):
        for side in range(2):
            @pl.when(has[side])
            def _():
                image_copy(step, 1 - side).wait_recv()

        acc[...] = jnp.zeros_like(acc)
        kind = KINDS[step]

        @pl.loop(0, views)
        def _(view):
            taps = [
                jnp.full((CHUNK, length_z), tap, F32).astype(kind)
                for tap in normalised(ny, view)
            ]
            weight = mine[pl.ds(view, 1), :]

            y_then_z(
                lambda j, at: img[step, j, at, :].astype(kind),
                own + 2 * halo, taps, False, bz[view],
            )

            if step == 0:
                for side in range(2):
                    @pl.when(has[side])
                    def _():
                        data_copy(view, 1 - side).wait_recv()
                        data_copy(view, side).wait_send()

                        @pl.when(view < views - AHEAD)
                        def _():
                            data_copy(view + AHEAD, side).start()

            for o in range(inner):
                blurred = dot(ax[view], half[o])
                scaled = wide[view, o].astype(F32) * weight
                ratio[o] = (scaled * pl.reciprocal(blurred, approx=True)).astype(BF)

            y_then_z(
                lambda j, at: ratio[j, at, :].astype(kind), inner, taps, True, bzt[view]
            )

            for o in range(own):
                acc[o] += jnp.log(dot(axt[view], half[o]))

        before = first if step == 0 else out
        out[...] = before[...] * jnp.exp(acc[...] * (1.0 / views))
        if step < ITERS - 1:
            img[step + 1, halo : halo + own] = out[...].astype(BF)
            for side in range(2):
                @pl.when(has[side])
                def _():
                    image_copy(step + 1, side).start()

    for side in range(2):
        @pl.when(has[side])
        def _():
            for step in range(ITERS):
                image_copy(step, side).wait_send()


def local(strips, estimate, views_data, kernel_x, kernel_y, kernel_z):
    views, own, length_x, length_z = views_data.shape
    ry = (kernel_y.shape[1] - 1) // 2
    inner = own + 2 * ry
    smem = pl.BlockSpec(memory_space=pltpu.SMEM)
    vmem = pl.BlockSpec(memory_space=pltpu.VMEM)
    hbm = pl.BlockSpec(memory_space=pl.ANY)
    plane = (length_x, length_z)
    flops = ITERS * views * (inner + own) * 2 * length_x * length_z * (length_x + length_z)
    return pl.pallas_call(
        functools.partial(kernel, strips),
        out_shape=jax.ShapeDtypeStruct(estimate.shape, F32),
        in_specs=[smem, smem, smem, hbm, hbm],
        out_specs=vmem,
        scratch_shapes=[
            pltpu.VMEM((ITERS, own + 4 * ry) + plane, BF),
            pltpu.VMEM((views, inner) + plane, BF),
            pltpu.VMEM((views, length_x, length_x), BF),
            pltpu.VMEM((views, length_x, length_x), BF),
            pltpu.VMEM((views, length_z, length_z), BF),
            pltpu.VMEM((views, length_z, length_z), BF),
            pltpu.VMEM((inner,) + plane, BF),
            pltpu.VMEM((inner,) + plane, BF),
            pltpu.VMEM((own,) + plane, F32),
            pltpu.VMEM((own,) + plane, F32),
            pltpu.VMEM((views, length_z), F32),
            pltpu.VMEM((strips, views, length_z), F32),
            pltpu.SemaphoreType.DMA,
            pltpu.SemaphoreType.DMA,
            pltpu.SemaphoreType.DMA((ITERS, 2)),
            pltpu.SemaphoreType.DMA((ITERS, 2)),
            pltpu.SemaphoreType.DMA((2, views)),
            pltpu.SemaphoreType.DMA((2, views)),
            pltpu.SemaphoreType.DMA((strips,)),
            pltpu.SemaphoreType.DMA((strips,)),
        ],
        compiler_params=pltpu.CompilerParams(
            collective_id=0, has_side_effects=True, vmem_limit_bytes=44 * 1024 * 1024
        ),
        cost_estimate=pl.CostEstimate(
            flops=flops, bytes_accessed=8 * 1024 * 1024, transcendentals=0
        ),
    )(kernel_x, kernel_y, kernel_z, estimate, views_data)


def solution(mesh):
    placed = (
        P(("blocks", "strip"), None, None),
        P(None, ("blocks", "strip"), None, None),
        P(),
        P(),
        P(),
    )
    return jax.shard_map(
        functools.partial(local, mesh.shape["strip"]),
        mesh=mesh,
        in_specs=placed,
        out_specs=P(("blocks", "strip"), None, None),
        check_vma=False,
    )
```

```python
import functools

import jax
import jax.numpy as jnp
from jax import lax
from jax.experimental import pallas as pl
from jax.experimental.pallas import tpu as pltpu
from jax.sharding import PartitionSpec as P

ITERS = 2
CHUNK = 16
BLOCK = 64
FIRST = 2
AHEAD = 5
MESH = pl.DeviceIdType.MESH
BF = jnp.bfloat16
F32 = jnp.float32


def normalised(taps_ref, view):
    taps = [taps_ref[view, t] for t in range(taps_ref.shape[1])]
    total = taps[0]
    for tap in taps[1:]:
        total = total + tap
    return [tap / total for tap in taps]


def band(taps, length, radius, start, size, flip):
    rows = lax.broadcasted_iota(jnp.int32, (size, length), 0) + start
    columns = lax.broadcasted_iota(jnp.int32, (size, length), 1)
    place = (rows - columns if flip else columns - rows) + radius
    total = jnp.zeros((size, length), F32)
    for t in range(2 * radius + 1):
        total = jnp.where(place == t, taps[t], total)
    return total.astype(BF)


def along_y(rows, taps, mirror):
    width = len(taps)
    outs = []
    for o in range(len(rows) - width + 1):
        terms = [
            taps[width - 1 - t if mirror else t] * rows[o + t] for t in range(width)
        ]
        while len(terms) > 1:
            terms = [a + b for a, b in zip(terms[::2], terms[1::2])] + (
                terms[-1:] if len(terms) % 2 else []
            )
        outs.append(terms[0])
    return outs


def dot(a, b):
    return jnp.dot(a, b, preferred_element_type=F32)


def kernel(
    strips, nx, ny, nz, est, data, out,
    img, wide, ax, axt, bz, bzt, half, ratio, saved, acc, first, mine, parts,
    local_sem, est_sem, img_send, img_recv, data_send, data_recv, sum_send, sum_recv,
):
    views, own, length_x, length_z = data.shape
    ry = (ny.shape[1] - 1) // 2
    rx = (nx.shape[1] - 1) // 2
    rz = (nz.shape[1] - 1) // 2
    halo = 2 * ry
    inner = own + 2 * ry
    me = lax.axis_index("strip")
    has = (me > 0, me < strips - 1)
    peer = (me - 1, me + 1)

    fetch_first = pltpu.make_async_copy(est, first, est_sem)
    fetch_first.start()
    barrier = pltpu.get_barrier_semaphore()

    @pl.loop(1, strips)
    def _(distance):
        pl.semaphore_signal(
            barrier,
            inc=1,
            device_id={"strip": lax.rem(me + distance, strips)},
            device_id_type=MESH,
        )

    fetch = pltpu.make_async_copy(data, wide.at[:, ry : ry + own], local_sem)
    fetch.start()
    fetch_first.wait()
    img[0, halo : halo + own] = first[...].astype(BF)
    for side in range(2):
        at_image = slice(0, halo) if side == 0 else slice(halo + own, 2 * halo + own)
        at_data = slice(0, ry) if side == 0 else slice(ry + own, 2 * ry + own)

        @pl.when(jnp.logical_not(has[side]))
        def _():
            for step in range(ITERS):
                img[step, at_image] = jnp.zeros((halo, length_x, length_z), BF)
            wide[:, at_data] = jnp.zeros((views, ry, length_x, length_z), BF)

    def image_copy(step, part, side):
        if side == 0:
            source, target = halo + part * ry, halo + own + part * ry
        else:
            source, target = halo + own - (1 + part) * ry, halo - (1 + part) * ry
        return pltpu.make_async_remote_copy(
            src_ref=img.at[step, pl.ds(source, ry)],
            dst_ref=img.at[step, pl.ds(target, ry)],
            send_sem=img_send.at[step, part, side],
            recv_sem=img_recv.at[step, part, 1 - side],
            device_id={"strip": peer[side]},
            device_id_type=MESH,
        )

    def send_image(step):
        for part in range(2):
            for side in range(2):
                @pl.when(has[side])
                def _():
                    image_copy(step, part, side).start()

    def wait_image(step, part):
        for side in range(2):
            @pl.when(has[side])
            def _():
                image_copy(step, part, 1 - side).wait_recv()

    def data_copy(view, side):
        if side == 0:
            source, target = pl.ds(0, ry), pl.ds(ry + own, ry)
        else:
            source, target = pl.ds(own - ry, ry), pl.ds(0, ry)
        return pltpu.make_async_remote_copy(
            src_ref=data.at[view, source],
            dst_ref=wide.at[view, target],
            send_sem=data_send.at[side, view],
            recv_sem=data_recv.at[1 - side, view],
            device_id={"strip": peer[side]},
            device_id_type=MESH,
        )

    def sum_copy(distance):
        return pltpu.make_async_remote_copy(
            src_ref=mine,
            dst_ref=parts.at[me],
            send_sem=sum_send.at[distance],
            recv_sem=sum_recv.at[distance],
            device_id={"strip": lax.rem(me + distance, strips)},
            device_id_type=MESH,
        )

    pl.semaphore_wait(barrier, strips - 1)
    send_image(0)

    for view in range(min(FIRST, views)):
        for side in range(2):
            @pl.when(has[side])
            def _():
                data_copy(view, side).start()

    fetch.wait()

    @pl.loop(0, views)
    def _(view):
        def add(chunk, total):
            at = pl.ds(pl.multiple_of(chunk * 32, 32), 32)
            for o in range(own):
                total = total + wide[view, ry + o, at, :].astype(F32)
            return total

        total = lax.fori_loop(
            0, length_x // 32, add, jnp.zeros((32, length_z), F32), unroll=2
        )
        mine[pl.ds(view, 1), :] = jnp.sum(total, axis=0, keepdims=True)

    @pl.loop(1, strips)
    def _(distance):
        sum_copy(distance).start()

    parts[me] = mine[...]

    @pl.loop(0, views)
    def _(view):
        taps_x, taps_z = normalised(nx, view), normalised(nz, view)
        for chunk in range(0, length_x, 64):
            at = pl.ds(chunk, 64)
            ax[view, at] = band(taps_x, length_x, rx, chunk, 64, False)
            axt[view, at] = band(taps_x, length_x, rx, chunk, 64, True)
        for chunk in range(0, length_z, 64):
            at = pl.ds(chunk, 64)
            bz[view, at] = band(taps_z, length_z, rz, chunk, 64, True)
            bzt[view, at] = band(taps_z, length_z, rz, chunk, 64, False)

    @pl.loop(1, strips)
    def _(distance):
        sum_copy(distance).wait()

    for view in range(min(FIRST, views), min(AHEAD, views)):
        for side in range(2):
            @pl.when(has[side])
            def _():
                data_copy(view, side).start()

    totals = jnp.sum(jnp.sum(parts[...], axis=0), axis=1, keepdims=True)
    weights = jnp.sum(totals, axis=0, keepdims=True) / (views * totals)
    mine[...] = jnp.broadcast_to(weights, mine.shape)

    def splat(view, kind):
        return [
            jnp.full((CHUNK, length_z), tap, F32).astype(kind)
            for tap in normalised(ny, view)
        ]

    def y_only(source, count, taps, mirror):
        @pl.loop(0, length_x // CHUNK, unroll=2)
        def _(chunk):
            at = pl.ds(pl.multiple_of(chunk * CHUNK, CHUNK), CHUNK)
            rows = [source(j, at).astype(F32) for j in range(count)]
            for o, value in enumerate(along_y(rows, taps, mirror)):
                half[o, at, :] = value.astype(BF)

    def y_then_z(runs, taps, mirror, matrix):
        @pl.loop(0, length_x // BLOCK, unroll=2)
        def _(block):
            starts = [
                pl.multiple_of(block * BLOCK + c, CHUNK) for c in range(0, BLOCK, CHUNK)
            ]
            pieces = []
            for start in starts:
                for run in runs:
                    rows = [source(pl.ds(start, CHUNK)) for source in run]
                    pieces += along_y(rows, taps, mirror)
            outs = len(pieces) // len(starts)
            result = dot(jnp.concatenate(pieces, axis=0), matrix).astype(BF)
            for index in range(len(pieces)):
                at = pl.ds(starts[index // outs], CHUNK)
                half[index % outs, at, :] = result[index * CHUNK : (index + 1) * CHUNK]

    def ratio_of(view, o, blurred):
        scaled = wide[view, o].astype(F32) * mine[pl.ds(view, 1), :]
        return (scaled * pl.reciprocal(blurred, approx=True)).astype(BF)

    def image_row(step, j):
        return lambda at: img[step, j, at, :]

    wait_image(0, 0)
    wait_image(0, 1)
    acc[...] = jnp.zeros_like(acc)

    @pl.loop(0, views)
    def _(view):
        taps = splat(view, F32)
        y_only(lambda j, at: img[0, j, at, :], own + 2 * halo, taps, False)
        for side in range(2):
            @pl.when(has[side])
            def _():
                data_copy(view, 1 - side).wait_recv()
                data_copy(view, side).wait_send()

                @pl.when(view < views - AHEAD)
                def _():
                    data_copy(view + AHEAD, side).start()

        for o in range(inner):
            second = dot(ax[view], half[o]).astype(BF)
            ratio[o] = ratio_of(view, o, dot(second, bz[view]))
        y_only(lambda j, at: ratio[j, at, :], inner, taps, True)
        for o in range(own):
            second = dot(axt[view], half[o]).astype(BF)
            acc[o] += jnp.log(dot(second, bzt[view]))

    out[...] = first[...] * jnp.exp(acc[...] * (1.0 / views))

    for step in range(1, ITERS):
        img[step, halo : halo + own] = out[...].astype(BF)
        send_image(step)
        acc[...] = jnp.zeros_like(acc)
        wait_image(step, 0)

        @pl.loop(0, views)
        def _(view):
            run = [image_row(step, j) for j in range(ry, inner + ry)]
            y_then_z([run], splat(view, BF), False, bz[view])
            for o in range(own):
                saved[view, o] = ratio_of(view, ry + o, dot(ax[view], half[o]))

        wait_image(step, 1)

        @pl.loop(0, views)
        def _(view):
            taps = splat(view, BF)
            low = [image_row(step, j) for j in range(3 * ry)]
            high = [image_row(step, j + ry + own) for j in range(3 * ry)]
            y_then_z([low, high], taps, False, bz[view])
            for o in range(2 * ry):
                row = o if o < ry else o + own
                ratio[o] = ratio_of(view, row, dot(ax[view], half[o]))
            run = [(lambda at, o=o: ratio[o, at, :]) for o in range(ry)]
            run += [(lambda at, o=o: saved[view, o, at, :]) for o in range(own)]
            run += [(lambda at, o=o: ratio[o, at, :]) for o in range(ry, 2 * ry)]
            y_then_z([run], taps, True, bzt[view])
            for o in range(own):
                acc[o] += jnp.log(dot(axt[view], half[o]))

        out[...] = out[...] * jnp.exp(acc[...] * (1.0 / views))

    for side in range(2):
        @pl.when(has[side])
        def _():
            for step in range(ITERS):
                for part in range(2):
                    image_copy(step, part, side).wait_send()


def local(strips, estimate, views_data, kernel_x, kernel_y, kernel_z):
    views, own, length_x, length_z = views_data.shape
    ry = (kernel_y.shape[1] - 1) // 2
    inner = own + 2 * ry
    smem = pl.BlockSpec(memory_space=pltpu.SMEM)
    vmem = pl.BlockSpec(memory_space=pltpu.VMEM)
    hbm = pl.BlockSpec(memory_space=pltpu.HBM)
    plane = (length_x, length_z)
    flops = ITERS * views * (inner + own) * 2 * length_x * length_z * (length_x + length_z)
    return pl.pallas_call(
        functools.partial(kernel, strips),
        out_shape=jax.ShapeDtypeStruct(estimate.shape, F32),
        in_specs=[smem, smem, smem, hbm, hbm],
        out_specs=vmem,
        scratch_shapes=[
            pltpu.VMEM((ITERS, own + 4 * ry) + plane, BF),
            pltpu.VMEM((views, inner) + plane, BF),
            pltpu.VMEM((views, length_x, length_x), BF),
            pltpu.VMEM((views, length_x, length_x), BF),
            pltpu.VMEM((views, length_z, length_z), BF),
            pltpu.VMEM((views, length_z, length_z), BF),
            pltpu.VMEM((inner,) + plane, BF),
            pltpu.VMEM((inner,) + plane, BF),
            pltpu.VMEM((views, own) + plane, BF),
            pltpu.VMEM((own,) + plane, F32),
            pltpu.VMEM((own,) + plane, F32),
            pltpu.VMEM((views, length_z), F32),
            pltpu.VMEM((strips, views, length_z), F32),
            pltpu.SemaphoreType.DMA,
            pltpu.SemaphoreType.DMA,
            pltpu.SemaphoreType.DMA((ITERS, 2, 2)),
            pltpu.SemaphoreType.DMA((ITERS, 2, 2)),
            pltpu.SemaphoreType.DMA((2, views)),
            pltpu.SemaphoreType.DMA((2, views)),
            pltpu.SemaphoreType.DMA((strips,)),
            pltpu.SemaphoreType.DMA((strips,)),
        ],
        compiler_params=pltpu.CompilerParams(
            collective_id=0, has_side_effects=True, vmem_limit_bytes=44 * 1024 * 1024
        ),
        cost_estimate=pl.CostEstimate(
            flops=flops, bytes_accessed=8 * 1024 * 1024, transcendentals=0
        ),
    )(kernel_x, kernel_y, kernel_z, estimate, views_data)


def solution(mesh):
    placed = (
        P(("blocks", "strip"), None, None),
        P(None, ("blocks", "strip"), None, None),
        P(),
        P(),
        P(),
    )
    return jax.shard_map(
        functools.partial(local, mesh.shape["strip"]),
        mesh=mesh,
        in_specs=placed,
        out_specs=P(("blocks", "strip"), None, None),
        check_vma=False,
    )
```

```python
import functools

import jax
import jax.numpy as jnp
from jax import lax
from jax.experimental import pallas as pl
from jax.experimental.pallas import tpu as pltpu
from jax.sharding import PartitionSpec as P

ITERS = 2
CHUNK = 16
BLOCK = 64
FIRST = 2
AHEAD = 5
MESH = pl.DeviceIdType.MESH
BF = jnp.bfloat16
F32 = jnp.float32


def normalised(taps_ref, view):
    taps = [taps_ref[view, t] for t in range(taps_ref.shape[1])]
    total = taps[0]
    for tap in taps[1:]:
        total = total + tap
    return [tap / total for tap in taps]


def band(taps, length, radius, start, size, flip):
    rows = lax.broadcasted_iota(jnp.int32, (size, length), 0) + start
    columns = lax.broadcasted_iota(jnp.int32, (size, length), 1)
    place = (rows - columns if flip else columns - rows) + radius
    total = jnp.zeros((size, length), F32)
    for t in range(2 * radius + 1):
        total = jnp.where(place == t, taps[t], total)
    return total.astype(BF)


def along_y(rows, taps, mirror):
    width = len(taps)
    outs = []
    for o in range(len(rows) - width + 1):
        terms = [
            taps[width - 1 - t if mirror else t] * rows[o + t] for t in range(width)
        ]
        while len(terms) > 1:
            terms = [a + b for a, b in zip(terms[::2], terms[1::2])] + (
                terms[-1:] if len(terms) % 2 else []
            )
        outs.append(terms[0])
    return outs


def dot(a, b):
    return jnp.dot(a, b, preferred_element_type=F32)


def kernel(
    strips, nx, ny, nz, est, data, out,
    img, wide, ax, axt, bz, bzt, half, ratio, saved, acc, first, mine, parts,
    local_sem, est_sem, img_send, img_recv, data_send, data_recv, sum_send, sum_recv,
):
    views, own, length_x, length_z = data.shape
    ry = (ny.shape[1] - 1) // 2
    rx = (nx.shape[1] - 1) // 2
    rz = (nz.shape[1] - 1) // 2
    halo = 2 * ry
    inner = own + 2 * ry
    me = lax.axis_index("strip")
    has = (me > 0, me < strips - 1)
    peer = (me - 1, me + 1)

    fetch_first = pltpu.make_async_copy(est, first, est_sem)
    fetch_first.start()
    barrier = pltpu.get_barrier_semaphore()

    @pl.loop(1, strips)
    def _(distance):
        pl.semaphore_signal(
            barrier,
            inc=1,
            device_id={"strip": lax.rem(me + distance, strips)},
            device_id_type=MESH,
        )

    fetch = pltpu.make_async_copy(data, wide.at[:, ry : ry + own], local_sem)
    fetch.start()
    fetch_first.wait()
    img[0, halo : halo + own] = first[...].astype(BF)
    for side in range(2):
        at_image = slice(0, halo) if side == 0 else slice(halo + own, 2 * halo + own)
        at_data = slice(0, ry) if side == 0 else slice(ry + own, 2 * ry + own)

        @pl.when(jnp.logical_not(has[side]))
        def _():
            for step in range(ITERS):
                img[step, at_image] = jnp.zeros((halo, length_x, length_z), BF)
            wide[:, at_data] = jnp.zeros((views, ry, length_x, length_z), BF)

    def image_copy(step, part, side):
        if side == 0:
            source, target = halo + part * ry, halo + own + part * ry
        else:
            source, target = halo + own - (1 + part) * ry, halo - (1 + part) * ry
        return pltpu.make_async_remote_copy(
            src_ref=img.at[step, pl.ds(source, ry)],
            dst_ref=img.at[step, pl.ds(target, ry)],
            send_sem=img_send.at[step, part, side],
            recv_sem=img_recv.at[step, part, 1 - side],
            device_id={"strip": peer[side]},
            device_id_type=MESH,
        )

    def send_image(step):
        for part in range(2):
            for side in range(2):
                @pl.when(has[side])
                def _():
                    image_copy(step, part, side).start()

    def wait_image(step, part):
        for side in range(2):
            @pl.when(has[side])
            def _():
                image_copy(step, part, 1 - side).wait_recv()

    def data_copy(view, side):
        if side == 0:
            source, target = pl.ds(0, ry), pl.ds(ry + own, ry)
        else:
            source, target = pl.ds(own - ry, ry), pl.ds(0, ry)
        return pltpu.make_async_remote_copy(
            src_ref=data.at[view, source],
            dst_ref=wide.at[view, target],
            send_sem=data_send.at[side, view],
            recv_sem=data_recv.at[1 - side, view],
            device_id={"strip": peer[side]},
            device_id_type=MESH,
        )

    def sum_copy(distance):
        return pltpu.make_async_remote_copy(
            src_ref=mine,
            dst_ref=parts.at[me],
            send_sem=sum_send.at[distance],
            recv_sem=sum_recv.at[distance],
            device_id={"strip": lax.rem(me + distance, strips)},
            device_id_type=MESH,
        )

    pl.semaphore_wait(barrier, strips - 1)
    send_image(0)

    for view in range(min(FIRST, views)):
        for side in range(2):
            @pl.when(has[side])
            def _():
                data_copy(view, side).start()

    fetch.wait()

    @pl.loop(0, views)
    def _(view):
        def add(chunk, total):
            at = pl.ds(pl.multiple_of(chunk * 32, 32), 32)
            for o in range(own):
                total = total + wide[view, ry + o, at, :].astype(F32)
            return total

        total = lax.fori_loop(
            0, length_x // 32, add, jnp.zeros((32, length_z), F32), unroll=2
        )
        mine[pl.ds(view, 1), :] = jnp.sum(total, axis=0, keepdims=True)

    @pl.loop(1, strips)
    def _(distance):
        sum_copy(distance).start()

    parts[me] = mine[...]

    @pl.loop(0, views)
    def _(view):
        taps_x, taps_z = normalised(nx, view), normalised(nz, view)
        for chunk in range(0, length_x, 64):
            at = pl.ds(chunk, 64)
            ax[view, at] = band(taps_x, length_x, rx, chunk, 64, False)
            axt[view, at] = band(taps_x, length_x, rx, chunk, 64, True)
        for chunk in range(0, length_z, 64):
            at = pl.ds(chunk, 64)
            bz[view, at] = band(taps_z, length_z, rz, chunk, 64, True)
            bzt[view, at] = band(taps_z, length_z, rz, chunk, 64, False)

    @pl.loop(1, strips)
    def _(distance):
        sum_copy(distance).wait()

    for view in range(min(FIRST, views), min(AHEAD, views)):
        for side in range(2):
            @pl.when(has[side])
            def _():
                data_copy(view, side).start()

    totals = jnp.sum(jnp.sum(parts[...], axis=0), axis=1, keepdims=True)
    weights = jnp.sum(totals, axis=0, keepdims=True) / (views * totals)
    mine[...] = jnp.broadcast_to(weights, mine.shape)

    def splat(view, kind):
        return [
            jnp.full((CHUNK, length_z), tap, F32).astype(kind)
            for tap in normalised(ny, view)
        ]

    def y_only(source, count, taps, mirror):
        @pl.loop(0, length_x // CHUNK, unroll=2)
        def _(chunk):
            at = pl.ds(pl.multiple_of(chunk * CHUNK, CHUNK), CHUNK)
            rows = [source(j, at).astype(F32) for j in range(count)]
            for o, value in enumerate(along_y(rows, taps, mirror)):
                half[o, at, :] = value.astype(BF)

    def y_then_z(runs, taps, mirror, matrix):
        @pl.loop(0, length_x // BLOCK, unroll=4)
        def _(block):
            starts = [
                pl.multiple_of(block * BLOCK + c, CHUNK) for c in range(0, BLOCK, CHUNK)
            ]
            pieces = []
            for start in starts:
                for run in runs:
                    rows = [source(pl.ds(start, CHUNK)) for source in run]
                    pieces += along_y(rows, taps, mirror)
            outs = len(pieces) // len(starts)
            result = dot(jnp.concatenate(pieces, axis=0), matrix).astype(BF)
            for index in range(len(pieces)):
                at = pl.ds(starts[index // outs], CHUNK)
                half[index % outs, at, :] = result[index * CHUNK : (index + 1) * CHUNK]

    def ratio_of(view, o, blurred):
        scaled = wide[view, o].astype(F32) * mine[pl.ds(view, 1), :]
        return (scaled * pl.reciprocal(blurred, approx=True)).astype(BF)

    def image_row(step, j):
        return lambda at: img[step, j, at, :]

    wait_image(0, 0)
    wait_image(0, 1)
    acc[...] = jnp.zeros_like(acc)

    @pl.loop(0, views)
    def _(view):
        taps = splat(view, F32)
        y_only(lambda j, at: img[0, j, at, :], own + 2 * halo, taps, False)
        for side in range(2):
            @pl.when(has[side])
            def _():
                data_copy(view, 1 - side).wait_recv()
                data_copy(view, side).wait_send()

                @pl.when(view < views - AHEAD)
                def _():
                    data_copy(view + AHEAD, side).start()

        for o in range(inner):
            second = dot(ax[view], half[o]).astype(BF)
            ratio[o] = ratio_of(view, o, dot(second, bz[view]))
        y_only(lambda j, at: ratio[j, at, :], inner, taps, True)
        for o in range(own):
            second = dot(axt[view], half[o]).astype(BF)
            acc[o] += jnp.log(dot(second, bzt[view]))

    out[...] = first[...] * jnp.exp(acc[...] * (1.0 / views))

    for step in range(1, ITERS):
        img[step, halo : halo + own] = out[...].astype(BF)
        send_image(step)
        acc[...] = jnp.zeros_like(acc)
        wait_image(step, 0)

        @pl.loop(0, views)
        def _(view):
            run = [image_row(step, j) for j in range(ry, inner + ry)]
            y_then_z([run], splat(view, BF), False, bz[view])
            for o in range(own):
                saved[view, o] = ratio_of(view, ry + o, dot(ax[view], half[o]))

        wait_image(step, 1)

        @pl.loop(0, views)
        def _(view):
            taps = splat(view, BF)
            low = [image_row(step, j) for j in range(3 * ry)]
            high = [image_row(step, j + ry + own) for j in range(3 * ry)]
            y_then_z([low, high], taps, False, bz[view])
            for o in range(2 * ry):
                row = o if o < ry else o + own
                ratio[o] = ratio_of(view, row, dot(ax[view], half[o]))
            run = [(lambda at, o=o: ratio[o, at, :]) for o in range(ry)]
            run += [(lambda at, o=o: saved[view, o, at, :]) for o in range(own)]
            run += [(lambda at, o=o: ratio[o, at, :]) for o in range(ry, 2 * ry)]
            y_then_z([run], taps, True, bzt[view])
            for o in range(own):
                acc[o] += jnp.log(dot(axt[view], half[o]))

        out[...] = out[...] * jnp.exp(acc[...] * (1.0 / views))

    for side in range(2):
        @pl.when(has[side])
        def _():
            for step in range(ITERS):
                for part in range(2):
                    image_copy(step, part, side).wait_send()


def local(strips, estimate, views_data, kernel_x, kernel_y, kernel_z):
    views, own, length_x, length_z = views_data.shape
    ry = (kernel_y.shape[1] - 1) // 2
    inner = own + 2 * ry
    smem = pl.BlockSpec(memory_space=pltpu.SMEM)
    vmem = pl.BlockSpec(memory_space=pltpu.VMEM)
    hbm = pl.BlockSpec(memory_space=pltpu.HBM)
    plane = (length_x, length_z)
    flops = ITERS * views * (inner + own) * 2 * length_x * length_z * (length_x + length_z)
    return pl.pallas_call(
        functools.partial(kernel, strips),
        out_shape=jax.ShapeDtypeStruct(estimate.shape, F32),
        in_specs=[smem, smem, smem, hbm, hbm],
        out_specs=vmem,
        scratch_shapes=[
            pltpu.VMEM((ITERS, own + 4 * ry) + plane, BF),
            pltpu.VMEM((views, inner) + plane, BF),
            pltpu.VMEM((views, length_x, length_x), BF),
            pltpu.VMEM((views, length_x, length_x), BF),
            pltpu.VMEM((views, length_z, length_z), BF),
            pltpu.VMEM((views, length_z, length_z), BF),
            pltpu.VMEM((inner,) + plane, BF),
            pltpu.VMEM((inner,) + plane, BF),
            pltpu.VMEM((views, own) + plane, BF),
            pltpu.VMEM((own,) + plane, F32),
            pltpu.VMEM((own,) + plane, F32),
            pltpu.VMEM((views, length_z), F32),
            pltpu.VMEM((strips, views, length_z), F32),
            pltpu.SemaphoreType.DMA,
            pltpu.SemaphoreType.DMA,
            pltpu.SemaphoreType.DMA((ITERS, 2, 2)),
            pltpu.SemaphoreType.DMA((ITERS, 2, 2)),
            pltpu.SemaphoreType.DMA((2, views)),
            pltpu.SemaphoreType.DMA((2, views)),
            pltpu.SemaphoreType.DMA((strips,)),
            pltpu.SemaphoreType.DMA((strips,)),
        ],
        compiler_params=pltpu.CompilerParams(
            collective_id=0, has_side_effects=True, vmem_limit_bytes=44 * 1024 * 1024
        ),
        cost_estimate=pl.CostEstimate(
            flops=flops, bytes_accessed=8 * 1024 * 1024, transcendentals=0
        ),
    )(kernel_x, kernel_y, kernel_z, estimate, views_data)


def solution(mesh):
    placed = (
        P(("blocks", "strip"), None, None),
        P(None, ("blocks", "strip"), None, None),
        P(),
        P(),
        P(),
    )
    return jax.shard_map(
        functools.partial(local, mesh.shape["strip"]),
        mesh=mesh,
        in_specs=placed,
        out_specs=P(("blocks", "strip"), None, None),
        check_vma=False,
    )
```
